32 devices in a mesh: tgt: 8 (over y, x, core), grp: 4 (over z).
Axes of the slice: x: 2, y: 2, z: 4, core: 2. Of those that a mesh axis runs over, the one named last changes fastest.
Arguments:
- targets: bfloat16 [8, 64, 64, 128], P('tgt', 'grp'), may hold values from -6 to 6
- partners: bfloat16 [8, 64, 64, 128], P('tgt'), may hold values from -6 to 6
- occupations: float32 [8], replicated, may hold values from 0.2 to 2
- slot_partner: int32 [8], replicated, may hold values from 0 to 7, each once
- screening: float32 [1], replicated, may hold values from 0.3 to 0.6
Outputs:
- exchange: float32 [8, 64, 64, 128], P('tgt', 'grp')
The draws below stay inside these ranges and needn't reach their ends.
Inputs may be any that keep to these rules, and one draw needn't show every extreme that they name: `slot_partner`: every partner id appears in exactly one slot.
All inputs are finite; a program needn't handle non-finite values.
Results may differ from the reference program's by a relative error of at most 0.011.
Values may be sent and summed in bfloat16 or wider, within the bound.
A program may use at most 64 MiB of HBM per device.

```python
import math
import jax
import jax.numpy as jnp
from jax import lax

NG = 64
NT = 8
NPART = 8


def level_of(own_key, extent, pieces, low, largest):
    level = 1.0
    for dim, parts in pieces:
        heights = jax.random.uniform(jax.random.fold_in(jax.random.fold_in(own_key, 6), dim), (parts,), jnp.float32, low / len(pieces), largest / len(pieces))
        level = level * jnp.repeat(jnp.exp(heights), extent[dim] // parts).reshape((-1,) + (1,) * (len(extent) - 1 - dim))
    return level


def noise(own_key, shape, scale, limit, shards=(), kind=jnp.bfloat16):
    gain = level_of(own_key, shape, shards, -0.22, 0.18) if shards else 1.0
    drawn = jax.random.normal(own_key, shape, jnp.float32) * scale * gain
    return jnp.minimum(jnp.maximum(drawn, -limit), limit).astype(kind)


def setup_inputs(seed: int = 0) -> dict:
    key_list = jax.random.split(jax.random.key(seed), 6)
    targets = noise(key_list[0], (NT, NG, NG, 2 * NG), 1.0, 6.0, ((0, 8), (1, 4)))
    partners = noise(key_list[1], (NPART, NG, NG, 2 * NG), 1.0, 6.0, ((0, 8),))
    occupations = jnp.clip(jnp.exp(jax.random.uniform(key_list[2], (NPART,), jnp.float32, math.log(0.2), math.log(2.0))), 0.2, 2.0)
    slot_partner = jax.random.permutation(key_list[3], NPART).astype(jnp.int32)
    screening = jnp.clip(jnp.exp(jax.random.uniform(key_list[4], (1,), jnp.float32, math.log(0.3), math.log(0.6))), 0.3, 0.6)
    return {"targets": targets, "partners": partners, "occupations": occupations, "slot_partner": slot_partner, "screening": screening}


coulomb_scale = 0.1

def fourier_table(points):
    indices = jnp.arange(points, dtype=jnp.int32)
    phases = indices[:, None] * indices[None, :] % points
    angles = phases.astype(jnp.float32) * (2.0 * math.pi / points)
    norm_factor = 1.0 / math.sqrt(points)
    return jnp.concatenate([jnp.cos(angles) * norm_factor, jnp.sin(angles) * norm_factor], axis=0).astype(jnp.bfloat16)

def coulomb_kernel(points, screening):
    indices = jnp.arange(points, dtype=jnp.int32)
    signed = jnp.where(indices < points // 2, indices, indices - points).astype(jnp.float32) * (2.0 * math.pi / points)
    squares = signed * signed
    wave_sq = squares[:, None, None] + squares[None, :, None] + squares[None, None, :]
    screen_wave = screening[0] * (2.0 * math.pi / points)
    inverse_sq = coulomb_scale / (wave_sq + screen_wave * screen_wave)
    return jnp.concatenate([inverse_sq, inverse_sq], axis=-1)

def slot_weights(occupations, slot_partner):
    ids = jnp.arange(occupations.shape[0], dtype=jnp.int32)
    match = slot_partner[:, None] == ids[None, :]
    return lax.optimization_barrier(jnp.sum(jnp.where(match, occupations[None, :], 0.0), axis=1))

def last_axis_matrix(tables, orient):
    points = tables.shape[1]
    cosine = tables[:points].T
    sine_part = tables[points:].T
    upper_rows = jnp.concatenate([cosine, -orient * sine_part], axis=1)
    bottom = jnp.concatenate([orient * sine_part, cosine], axis=1)
    return jnp.concatenate([upper_rows, bottom], axis=0)

def combine(cos_part, sin_part, orient, points):
    real_part = cos_part[..., :points] + orient * sin_part[..., points:]
    imag_part = cos_part[..., points:] - orient * sin_part[..., :points]
    return jnp.concatenate([real_part, imag_part], axis=-1).astype(jnp.bfloat16)

def section_last(field, tables, orient):
    points = tables.shape[1]
    field = lax.optimization_barrier(field)
    matrix = last_axis_matrix(tables, orient).astype(jnp.float32)
    flat = field.reshape(-1, 2 * points).astype(jnp.float32)
    result = jnp.dot(flat, matrix, precision=lax.Precision.HIGHEST, preferred_element_type=jnp.float32)
    return result.reshape(field.shape).astype(jnp.bfloat16)

def section_middle(field, tables, orient):
    points = tables.shape[1]
    field = lax.optimization_barrier(field)
    stacked = jnp.einsum('ky,bxyw->bxkw', tables.astype(jnp.float32), field.astype(jnp.float32), precision=lax.Precision.HIGHEST)
    return combine(stacked[:, :, :points], stacked[:, :, points:], orient, points)

def section_first(field, tables, orient):
    points = tables.shape[1]
    field = lax.optimization_barrier(field)
    stacked = jnp.einsum('kx,bxyw->bkyw', tables.astype(jnp.float32), field.astype(jnp.float32), precision=lax.Precision.HIGHEST)
    return combine(stacked[:, :points], stacked[:, points:], orient, points)

def exchange_term(targets, partner, weight, tables, kernel):
    points = tables.shape[1]
    part_real = partner[..., :points].astype(jnp.float32)
    part_imag = partner[..., points:].astype(jnp.float32)
    tgt_real = targets[..., :points].astype(jnp.float32)
    tgt_imag = targets[..., points:].astype(jnp.float32)
    density = jnp.concatenate([part_real * tgt_real + part_imag * tgt_imag, part_real * tgt_imag - part_imag * tgt_real], axis=-1).astype(jnp.bfloat16)
    spectrum = section_first(section_middle(section_last(density, tables, 1.0), tables, 1.0), tables, 1.0)
    spectrum = lax.optimization_barrier(spectrum)
    scaled = (spectrum.astype(jnp.float32) * kernel).astype(jnp.bfloat16)
    potential = section_last(section_middle(section_first(scaled, tables, -1.0), tables, -1.0), tables, -1.0)
    potential = lax.optimization_barrier(potential)
    pot_real = potential[..., :points].astype(jnp.float32)
    pot_imag = potential[..., points:].astype(jnp.float32)
    real_part = pot_real * part_real - pot_imag * part_imag
    imag_part = pot_real * part_imag + pot_imag * part_real
    return weight * jnp.concatenate([real_part, imag_part], axis=-1)

def reference(targets, partners, occupations, slot_partner, screening):
    points = targets.shape[1]
    tables = fourier_table(points)
    kernel = coulomb_kernel(points, screening)
    slot_weight = slot_weights(occupations, slot_partner)

    def advance(totals, inputs):
        partner, weight = inputs
        return (totals + exchange_term(targets, partner, weight, tables, kernel), None)
    totals, _ = lax.scan(advance, jnp.zeros(targets.shape, jnp.float32), (partners, slot_weight))
    return -totals
```

```python
import functools
import math

import jax
import jax.numpy as jnp
import numpy as np
from jax import lax
from jax.experimental import pallas as pl
from jax.experimental.pallas import tpu as pltpu
from jax.sharding import PartitionSpec as P

coulomb_scale = 0.1
MESH = pl.DeviceIdType.MESH


def tables(points):
    indices = np.arange(points)
    angles = (indices[:, None] * indices[None, :] % points) * (2.0 * math.pi / points)
    norm = 1.0 / math.sqrt(points)
    bf16 = lambda a: a.astype(np.float32).astype(jnp.bfloat16).astype(np.float32)
    return bf16(np.cos(angles) * norm), bf16(np.sin(angles) * norm)


def matrices(points):
    c, s = tables(points)
    n = points
    fz = np.block([[c, -s], [s, c]])
    fz = np.concatenate([fz, fz[:, n:], -fz[:, :n]], axis=1)
    fy = np.block([[c, s], [-s, c]])
    iy = np.block([[c, -s], [s, c]])
    iz = np.block([[c, s], [-s, c]])
    iz = np.concatenate([iz, iz[:, n:], iz[:, :n]], axis=1)
    return [m.astype(jnp.bfloat16) for m in (fz, fy, iy, iz)]


def compute_kernel(n, tgt_ref, part_ref, fz_ref, fy_ref, iy_ref, iz_ref, occ_ref, slot_ref, scr_ref,
                   out_ref, s1, s2):
    f32, bf16 = jnp.float32, jnp.bfloat16
    R = tgt_ref.shape[0]
    w = 2 * n
    ld = s1.shape[0] // w
    G = 4
    weight = -occ_ref[slot_ref[lax.axis_index("tgt")]]
    unit = 2.0 * math.pi / n
    kappa = scr_ref[0] * unit
    kappa_sq = kappa * kappa
    signed = lambda i: jnp.where(i < n // 2, i, i - n).astype(f32) * unit
    lane = lax.broadcasted_iota(jnp.int32, (n, w), 1)
    gx = signed(lax.broadcasted_iota(jnp.int32, (n, w), 0))
    gz = signed(lane % n)
    base = gx * gx + gz * gz + kappa_sq
    low = lax.broadcasted_iota(jnp.int32, (G * n, w), 1) < n

    def dot(a, b):
        return jnp.dot(a, b, preferred_element_type=f32)

    def partner_parts(rows):
        q = part_ref[rows, :].astype(f32)
        turned = pltpu.roll(q, n, 1)
        return jnp.where(low, q, turned), jnp.where(low, -turned, q)

    for r in range(R):

        @pl.loop(0, n // G)
        def _(i):
            rows = pl.ds(pl.multiple_of(i * (G * n), G * n), G * n)
            t = tgt_ref[r, rows, :].astype(f32)
            q1, q2 = partner_parts(rows)
            density = (q1 * t - q2 * pltpu.roll(t, n, 1)).astype(bf16)
            f = dot(density, fz_ref[...]).astype(bf16)
            for a in range(0, G, 2):
                stack = [
                    jnp.concatenate([f[b * n:(b + 1) * n, :w], f[b * n:(b + 1) * n, w:]], axis=0)
                    for b in (a, a + 1)
                ]
                o = dot(fy_ref[...], jnp.concatenate(stack, axis=1))
                for b in range(2):
                    s1[pl.ds(i * G + a + b, w, stride=ld), :] = o[:, b * w:(b + 1) * w]

        @pl.loop(0, n // G)
        def _(i):
            for a in range(0, G, 2):
                stack, kern = [], []
                for b in range(2):
                    ky = i * G + a + b
                    top = s1[pl.ds(pl.multiple_of(ky * ld, 8), n), :]
                    bottom = s1[pl.ds(pl.multiple_of((ky + n) * ld, 8), n), :]
                    stack.append(jnp.concatenate([top, bottom], axis=0).astype(bf16))
                    gy = signed(ky)
                    k = coulomb_scale / (base + gy * gy)
                    kern.append(jnp.concatenate([k, k], axis=0))
                spectrum = dot(fy_ref[...], jnp.concatenate(stack, axis=1))
                scaled = (spectrum * jnp.concatenate(kern, axis=1)).astype(bf16)
                o = dot(iy_ref[...], scaled)
                for b in range(2):
                    s2[pl.ds(i * G + a + b, w, stride=ld), :] = o[:, b * w:(b + 1) * w]

        @pl.loop(0, n // G)
        def _(i):
            rows = pl.ds(pl.multiple_of(i * (G * n), G * n), G * n)
            parts = []
            for a in range(0, G, 2):
                stack = []
                for b in range(2):
                    x = i * G + a + b
                    top = s2[pl.ds(pl.multiple_of(x * ld, 8), n), :]
                    bottom = s2[pl.ds(pl.multiple_of((x + n) * ld, 8), n), :]
                    stack.append(jnp.concatenate([top, bottom], axis=0).astype(bf16))
                o = dot(iy_ref[:n, :], jnp.concatenate(stack, axis=1)).astype(bf16)
                parts += [o[:, :w], o[:, w:]]
            potential = dot(jnp.concatenate(parts, axis=0), iz_ref[...])
            q1, q2 = partner_parts(rows)
            out_ref[r, rows, :] = (
                weight * (potential[:, :w] * q1 + potential[:, w:] * q2)
            ).astype(bf16)


def gather_kernel(NT, NG, src, out, p1_send, p1_recv, p2_send, p2_recv, sib_send, sib_recv):
    R, C = NT // NG, NT // 2
    t, g = lax.axis_index("tgt"), lax.axis_index("grp")
    c, p = t // 2, t % 2
    own_set = t // R
    sibling = c * 2 + 1 - p
    inside = own_set == g

    barrier = pltpu.get_barrier_semaphore()
    for r in range(R):
        for h in range(NG):

            @pl.when(jnp.logical_not(inside & (t == g * R + r) & (h == g)))
            def _():
                pl.semaphore_signal(barrier, inc=1, device_id=(g * R + r, h), device_id_type=MESH)

    for m in range(1, C):
        pl.semaphore_signal(barrier, inc=1, device_id=((c + C - m) % C * 2 + p, g), device_id_type=MESH)
    pl.semaphore_signal(barrier, inc=1, device_id=(sibling, g), device_id_type=MESH)

    @pl.when(inside)
    def _():
        pl.semaphore_wait(barrier, NT - 1 + C)

    @pl.when(jnp.logical_not(inside))
    def _():
        pl.semaphore_wait(barrier, NT + C)

    def spread(j):
        return pltpu.make_async_remote_copy(
            src_ref=src.at[j], dst_ref=out.at[t % R, g, j], send_sem=p1_send.at[j],
            recv_sem=p1_recv.at[t % R, g], device_id=(j, own_set), device_id_type=MESH)

    def is_self(j):
        return inside & (t == j)

    own = pltpu.make_async_copy(src.at[t], out.at[t % R, g, t], p1_recv.at[t % R, g])
    for m in range(NT):
        j = (t + m) % NT
        if m == 0:

            @pl.when(inside)
            def _():
                own.start()

            @pl.when(jnp.logical_not(inside))
            def _():
                spread(j).start()
        else:
            spread(j).start()

    def peer(r, m):
        return pltpu.make_async_remote_copy(
            src_ref=out.at[r, :, t], dst_ref=out.at[r, :, t], send_sem=p2_send.at[r, m],
            recv_sem=p2_recv.at[r, m], device_id=((c + m) % C * 2 + p, g), device_id_type=MESH)

    def to_sibling(r, m):
        j = (c + C - m) % C * 2 + p
        return pltpu.make_async_remote_copy(
            src_ref=out.at[r, :, j], dst_ref=out.at[r, :, j], send_sem=sib_send.at[r, m],
            recv_sem=sib_recv.at[r, m], device_id=(sibling, g), device_id_type=MESH)

    for r in range(R):
        for h in range(NG):
            piece = out.at[r, h, t]
            pltpu.make_async_copy(piece, piece, p1_recv.at[r, h]).wait()
        for m in range(1, C):
            peer(r, m).start()
        to_sibling(r, 0).start()
    for r in range(R):
        for m in range(1, C):
            peer(r, m).wait_recv()
            to_sibling(r, m).start()
    for r in range(R):
        for m in range(C):
            to_sibling(r, m).wait()
            if m:
                peer(r, m).wait_send()
    for m in range(1, NT):
        spread((t + m) % NT).wait_send()

    @pl.when(jnp.logical_not(inside))
    def _():
        spread(t).wait_send()


def reduce_kernel(NT, NG, part, out, sib, acc, inbox, fin, final, s_send, s_recv, r_send, r_recv, f_send, f_recv):
    f32, bf16 = jnp.float32, jnp.bfloat16
    R, C = NT // NG, NT // 2
    t, g = lax.axis_index("tgt"), lax.axis_index("grp")
    c, p = t // 2, t % 2
    own_set = t // R
    sibling = c * 2 + 1 - p
    inside = own_set == g

    barrier = pltpu.get_barrier_semaphore()
    for m in range(NT):
        j = (t + m) % NT
        if m == 0:

            @pl.when(jnp.logical_not(inside))
            def _():
                pl.semaphore_signal(barrier, inc=1, device_id=(j, own_set), device_id_type=MESH)
        else:
            pl.semaphore_signal(barrier, inc=1, device_id=(j, own_set), device_id_type=MESH)
    for m in range(1, C):
        pl.semaphore_signal(barrier, inc=1, device_id=((c + C - m) % C * 2 + p, g), device_id_type=MESH)
    pl.semaphore_signal(barrier, inc=1, device_id=(sibling, g), device_id_type=MESH)

    @pl.when(inside)
    def _():
        pl.semaphore_wait(barrier, NT - 1 + C)

    @pl.when(jnp.logical_not(inside))
    def _():
        pl.semaphore_wait(barrier, NT + C)

    def to_sibling(r, m):
        d = (c + m) % C
        return pltpu.make_async_remote_copy(
            src_ref=part.at[r, :, d * 2 + 1 - p], dst_ref=sib.at[r, m], send_sem=s_send.at[r, m],
            recv_sem=s_recv.at[r, m], device_id=(sibling, g), device_id_type=MESH)

    def peer(r, m):
        return pltpu.make_async_remote_copy(
            src_ref=acc.at[r, m], dst_ref=inbox.at[r, m], send_sem=r_send.at[r, m],
            recv_sem=r_recv.at[r, m], device_id=((c + m) % C * 2 + p, g), device_id_type=MESH)

    def to_owner(r, h):
        return pltpu.make_async_remote_copy(
            src_ref=fin.at[r, h], dst_ref=final.at[t], send_sem=f_send.at[r, h],
            recv_sem=f_recv.at[t], device_id=(g * R + r, h), device_id_type=MESH)

    order = list(range(1, C)) + [0]
    for r in range(R):
        for m in order:
            to_sibling(r, m).start()
    for r in range(R):
        for m in order:
            to_sibling(r, m).wait_recv()
            mine = part[r, :, (c + m) % C * 2 + p]
            acc[r, m] = (mine.astype(f32) + sib[r, m].astype(f32)).astype(bf16)
            if m:
                peer(r, m).start()
    own = pltpu.make_async_copy(fin.at[t % R, g], final.at[t], f_recv.at[t])
    for r in range(R):
        for m in range(1, C):
            peer(r, m).wait_recv()
        total = acc[r, 0].astype(f32)
        for m in range(1, C):
            total = total + inbox[r, m].astype(f32)
        fin[r] = total.astype(bf16)
        for h in range(NG):
            here = inside & (t == g * R + r) & (g == h)

            @pl.when(here)
            def _():
                own.start()

            @pl.when(jnp.logical_not(here))
            def _():
                to_owner(r, h).start()

    for m in range(NT):
        j = (t + m) % NT
        piece = final.at[j]
        pltpu.make_async_copy(piece, piece, f_recv.at[j]).wait()
        out[j] = final[j].astype(f32)
    for r in range(R):
        for m in range(C):
            to_sibling(r, m).wait_send()
            if m:
                peer(r, m).wait_send()
        for h in range(NG):
            here = inside & (t == g * R + r) & (g == h)

            @pl.when(jnp.logical_not(here))
            def _():
                to_owner(r, h).wait_send()


def body(targets, partners, occupations, slot_partner, screening):
    NT, NG = lax.axis_size("tgt"), lax.axis_size("grp")
    R, C = NT // NG, NT // 2
    _, planes, n, w = targets.shape
    rows = planes * n // NT
    piece = (rows, w)
    vmem = pl.BlockSpec(memory_space=pltpu.VMEM)
    smem = pl.BlockSpec(memory_space=pltpu.SMEM)
    dma = pltpu.SemaphoreType.DMA
    bf16 = jnp.bfloat16
    limit = 48 << 20

    gathered = pl.pallas_call(
        functools.partial(gather_kernel, NT, NG),
        out_shape=jax.ShapeDtypeStruct((R, NG, NT) + piece, bf16),
        in_specs=[vmem],
        out_specs=vmem,
        scratch_shapes=[dma((NT,)), dma((R, NG)), dma((R, C)), dma((R, C)), dma((R, C)), dma((R, C))],
        compiler_params=pltpu.CompilerParams(
            collective_id=0, has_side_effects=True, vmem_limit_bytes=limit),
    )(targets.reshape((NT,) + piece))

    mats = [jnp.asarray(m) for m in matrices(n)]
    ld = n + 8
    partial = pl.pallas_call(
        functools.partial(compute_kernel, n),
        out_shape=jax.ShapeDtypeStruct((R, n * n, w), bf16),
        in_specs=[vmem] * 6 + [smem] * 3,
        out_specs=vmem,
        scratch_shapes=[pltpu.VMEM((w * ld, w), jnp.float32)] * 2,
        compiler_params=pltpu.CompilerParams(vmem_limit_bytes=limit),
    )(gathered.reshape(R, n * n, w), partners.reshape(n * n, w), *mats,
      occupations, slot_partner, screening)

    out = pl.pallas_call(
        functools.partial(reduce_kernel, NT, NG),
        out_shape=jax.ShapeDtypeStruct((NT,) + piece, jnp.float32),
        in_specs=[vmem],
        out_specs=vmem,
        scratch_shapes=[
            pltpu.VMEM((R, C, NG) + piece, bf16),
            pltpu.VMEM((R, C, NG) + piece, bf16),
            pltpu.VMEM((R, C, NG) + piece, bf16),
            pltpu.VMEM((R, NG) + piece, bf16),
            pltpu.VMEM((NT,) + piece, bf16),
            dma((R, C)), dma((R, C)), dma((R, C)), dma((R, C)), dma((R, NG)), dma((NT,)),
        ],
        compiler_params=pltpu.CompilerParams(
            collective_id=1, has_side_effects=True, vmem_limit_bytes=limit),
    )(partial.reshape((R, NG, NT) + piece))
    return out.reshape(targets.shape)


def solution(mesh):
    in_specs = (P("tgt", "grp", None, None), P("tgt", None, None, None), P(), P(), P())
    out_specs = P("tgt", "grp", None, None)
    return jax.shard_map(body, mesh=mesh, in_specs=in_specs, out_specs=out_specs, check_vma=False)
```

```python
import functools
import math

import jax
import jax.numpy as jnp
import numpy as np
from jax import lax
from jax.experimental import pallas as pl
from jax.experimental.pallas import tpu as pltpu
from jax.sharding import PartitionSpec as P

coulomb_scale = 0.1
MESH = pl.DeviceIdType.MESH


def tables(points):
    indices = np.arange(points)
    angles = (indices[:, None] * indices[None, :] % points) * (2.0 * math.pi / points)
    norm = 1.0 / math.sqrt(points)
    bf16 = lambda a: a.astype(np.float32).astype(jnp.bfloat16).astype(np.float32)
    return bf16(np.cos(angles) * norm), bf16(np.sin(angles) * norm)


def matrices(points):
    c, s = tables(points)
    n = points
    fz = np.block([[c, -s], [s, c]])
    fz = np.concatenate([fz, fz[:, n:], -fz[:, :n]], axis=1)
    fy = np.block([[c, s], [-s, c]])
    iy = np.block([[c, -s], [s, c]])
    iz = np.block([[c, s], [-s, c]])
    iz = np.concatenate([iz, iz[:, n:], iz[:, :n]], axis=1)
    return [m.astype(jnp.bfloat16) for m in (fz, fy, iy, iz)]


def exchange_kernel(NT, NG, src, part_hbm, fz_ref, fy_ref, iy_ref, iz_ref, occ_ref, slot_ref, scr_ref, out,
                    gat, partner, q1_ref, q2_ref, kern_ref, s1, s2, part, sib, acc, inbox, fin, final,
                    load_sem, p1_send, p1_recv, p2_send, p2_recv, b_send, b_recv,
                    s_send, s_recv, r_send, r_recv, f_send, f_recv):
    f32, bf16 = jnp.float32, jnp.bfloat16
    R, C = NT // NG, NT // 2
    n = kern_ref.shape[0]
    w = 2 * n
    P2 = 2 * src.shape[1]
    k = P2 // n
    ld = s1.shape[0] // w
    t, g = lax.axis_index("tgt"), lax.axis_index("grp")
    c, p = t // 2, t % 2
    own_set = t // R
    sibling = c * 2 + 1 - p
    inside = own_set == g

    load = pltpu.make_async_copy(part_hbm, partner, load_sem)
    load.start()

    barrier = pltpu.get_barrier_semaphore()

    def greet(*device):
        pl.semaphore_signal(barrier, inc=1, device_id=device, device_id_type=MESH)

    for m in range(NT):
        if m == 0:
            pl.when(jnp.logical_not(inside))(lambda: greet(t, own_set))
        else:
            greet((t + m) % NT, own_set)
    for r in range(R):
        for h in range(NG):
            here = (t == g * R + r) & (g == h)
            pl.when(jnp.logical_not(here))(lambda: greet(g * R + r, h))
    for m in range(1, C):
        greet((c + m) % C * 2 + p, g)
    greet(sibling, g)

    @pl.when(inside)
    def _():
        pl.semaphore_wait(barrier, 2 * NT - 2 + C)

    @pl.when(jnp.logical_not(inside))
    def _():
        pl.semaphore_wait(barrier, 2 * NT + C)

    def remote(a, b, send, recv, *device):
        return pltpu.make_async_remote_copy(
            src_ref=a, dst_ref=b, send_sem=send, recv_sem=recv, device_id=device, device_id_type=MESH)

    def spread(j):
        return remote(src.at[j], gat.at[t % R, g, j // 2, j % 2], p1_send.at[j], p1_recv.at[t % R, g], j, own_set)

    own_piece = pltpu.make_async_copy(src.at[t], gat.at[t % R, g, c, p], p1_recv.at[t % R, g])
    for m in range(1, NT):
        spread((t + m) % NT).start()
    pl.when(inside)(own_piece.start)
    pl.when(jnp.logical_not(inside))(lambda: spread(t).start())

    def peer(r, m):
        ref = gat.at[r, :, c, p]
        return remote(ref, ref, p2_send.at[r, m], p2_recv.at[r, m], (c + m) % C * 2 + p, g)

    def forward(r, m):
        ref = gat.at[r, :, (c + C - m) % C, p]
        return remote(ref, ref, b_send.at[r, m], b_recv.at[r, m], sibling, g)

    def spread_in_plane(r):
        for h in range(NG):
            piece = gat.at[r, h, c, p]
            pltpu.make_async_copy(piece, piece, p1_recv.at[r, h]).wait()
        for m in range(1, C):
            peer(r, m).start()
        forward(r, 0).start()

    unit = 2.0 * math.pi / n
    kappa = scr_ref[0] * unit
    weight = -occ_ref[slot_ref[t]]
    signed = lambda i: jnp.where(i < n // 2, i, i - n).astype(f32) * unit
    lane = lax.broadcasted_iota(jnp.int32, (n, w), 1)
    gx = signed(lax.broadcasted_iota(jnp.int32, (n, w), 0))
    gz = signed(lane % n)
    base = gx * gx + gz * gz + kappa * kappa

    @pl.loop(0, n)
    def _(ky):
        gy = signed(ky)
        kern_ref[ky] = coulomb_scale / (base + gy * gy)

    load.wait()
    low = lax.broadcasted_iota(jnp.int32, (P2, w), 1) < n

    @pl.loop(0, C)
    def _(cc):
        for h in range(NG):
            q = partner[h, cc].astype(f32)
            turned = pltpu.roll(q, n, 1)
            q1_ref[h, cc] = jnp.where(low, q, turned).astype(bf16)
            q2_ref[h, cc] = jnp.where(low, -turned, q).astype(bf16)

    def dot(a, b):
        return jnp.dot(a, b, preferred_element_type=f32)

    def both(ref, h, cc):
        return jnp.concatenate([ref[h, cc], ref[h + 1, cc]], axis=0).astype(f32)

    def stage_one(r, cc):
        @pl.loop(0, NG // 2)
        def _(hh):
            h = hh * 2
            v = jnp.concatenate([gat[r, h, cc].reshape(P2, w), gat[r, h + 1, cc].reshape(P2, w)], axis=0).astype(f32)
            density = (both(q1_ref, h, cc) * v - both(q2_ref, h, cc) * pltpu.roll(v, n, 1)).astype(bf16)
            f = dot(density, fz_ref[...]).astype(bf16)
            for a in range(0, 2 * k, 2):
                stack = [
                    jnp.concatenate([f[b * n:(b + 1) * n, :w], f[b * n:(b + 1) * n, w:]], axis=0)
                    for b in (a, a + 1)
                ]
                o = dot(fy_ref[...], jnp.concatenate(stack, axis=1))
                for b in range(2):
                    x = ((h + (a + b) // k) * C + cc) * k + (a + b) % k
                    s1[pl.ds(x, w, stride=ld), :] = o[:, b * w:(b + 1) * w]

    def rows_of(s, i):
        top = s[pl.ds(pl.multiple_of(i * ld, 8), n), :]
        bottom = s[pl.ds(pl.multiple_of((i + n) * ld, 8), n), :]
        return jnp.concatenate([top, bottom], axis=0).astype(bf16)

    def stage_two():
        G = 8

        @pl.loop(0, n // G)
        def _(i):
            for a in range(0, G, 2):
                ky = i * G + a
                spectrum = dot(fy_ref[...], jnp.concatenate([rows_of(s1, ky), rows_of(s1, ky + 1)], axis=1))
                half = jnp.concatenate([kern_ref[ky], kern_ref[ky + 1]], axis=1)
                scaled = (spectrum * jnp.concatenate([half, half], axis=0)).astype(bf16)
                o = dot(iy_ref[...], scaled)
                for b in range(2):
                    s2[pl.ds(ky + b, w, stride=ld), :] = o[:, b * w:(b + 1) * w]

    def stage_three(r, cc):
        @pl.loop(0, NG // 2)
        def _(hh):
            h = hh * 2
            parts = []
            for a in range(0, 2 * k, 2):
                stack = [
                    rows_of(s2, ((h + e // k) * C + cc) * k + e % k) for e in (a, a + 1)
                ]
                o = dot(iy_ref[:n, :], jnp.concatenate(stack, axis=1)).astype(bf16)
                parts += [o[:, :w], o[:, w:]]
            potential = dot(jnp.concatenate(parts, axis=0), iz_ref[...])
            result = weight * (potential[:, :w] * both(q1_ref, h, cc) + potential[:, w:] * both(q2_ref, h, cc))
            result = result.astype(bf16)
            part[r, h, cc] = result[:P2].reshape(2, P2 // 2, w)
            part[r, h + 1, cc] = result[P2:].reshape(2, P2 // 2, w)

    def out_sibling(r, m):
        return remote(part.at[r, :, (c + m) % C, 1 - p], sib.at[r, m], s_send.at[r, m], s_recv.at[r, m], sibling, g)

    def out_peer(r, m):
        return remote(acc.at[r, m], inbox.at[r, m], r_send.at[r, m], r_recv.at[r, m], (c + m) % C * 2 + p, g)

    def to_owner(r, h):
        return remote(fin.at[r, h], final.at[t], f_send.at[r, h], f_recv.at[t], g * R + r, h)

    def add_sibling(r, m):
        out_sibling(r, m).wait_recv()
        mine = part[r, :, (c + m) % C, p]
        acc[r, m] = (mine.astype(f32) + sib[r, m].astype(f32)).astype(bf16)

    own_sum = pltpu.make_async_copy(fin.at[t % R, g], final.at[t], f_recv.at[t])

    def finish(r):
        for m in range(1, C):
            out_peer(r, m).wait_recv()
        total = acc[r, 0].astype(f32)
        for m in range(1, C):
            total = total + inbox[r, m].astype(f32)
        fin[r] = total.astype(bf16)
        for h in range(NG):
            here = (t == g * R + r) & (g == h)
            pl.when(here)(own_sum.start)
            pl.when(jnp.logical_not(here))(lambda: to_owner(r, h).start())

    spread_in_plane(0)
    for r in range(R):

        @pl.loop(1, C)
        def _(m):
            peer(r, m).wait_recv()
            forward(r, m).start()
            forward(r, m - 1).wait_recv()
            stage_one(r, (c + C - (m - 1)) % C)

        if r + 1 < R:
            spread_in_plane(r + 1)
        forward(r, C - 1).wait_recv()
        stage_one(r, (c + 1) % C)
        if r:
            finish(r - 1)
        stage_two()

        stage_three(r, (c + 1) % C)
        out_sibling(r, 1).start()

        @pl.loop(2, C)
        def _(m):
            stage_three(r, (c + m) % C)
            out_sibling(r, m).start()
            add_sibling(r, m - 1)
            out_peer(r, m - 1).start()

        stage_three(r, c)
        out_sibling(r, 0).start()
        add_sibling(r, C - 1)
        out_peer(r, C - 1).start()
        add_sibling(r, 0)
    finish(R - 1)

    for m in range(NT):
        j = (t + m) % NT
        piece = final.at[j]
        pltpu.make_async_copy(piece, piece, f_recv.at[j]).wait()
        out[j] = final[j].astype(f32)
    for m in range(1, NT):
        spread((t + m) % NT).wait_send()
    pl.when(jnp.logical_not(inside))(lambda: spread(t).wait_send())
    for r in range(R):
        for m in range(C):
            forward(r, m).wait_send()
            out_sibling(r, m).wait_send()
            if m:
                peer(r, m).wait_send()
                out_peer(r, m).wait_send()
        for h in range(NG):
            here = (t == g * R + r) & (g == h)
            pl.when(jnp.logical_not(here))(lambda: to_owner(r, h).wait_send())


def body(targets, partners, occupations, slot_partner, screening):
    NT, NG = lax.axis_size("tgt"), lax.axis_size("grp")
    R, C = NT // NG, NT // 2
    _, planes, n, w = targets.shape
    rows = planes * n // NT
    piece = (rows, w)
    anywhere = pl.BlockSpec(memory_space=pl.ANY)
    vmem = pl.BlockSpec(memory_space=pltpu.VMEM)
    smem = pl.BlockSpec(memory_space=pltpu.SMEM)
    dma = pltpu.SemaphoreType.DMA
    bf16, f32 = jnp.bfloat16, jnp.float32
    mats = [jnp.asarray(m) for m in matrices(n)]
    ld = n + 8
    field = (NG, C, 2 * rows, w)
    out = pl.pallas_call(
        functools.partial(exchange_kernel, NT, NG),
        out_shape=jax.ShapeDtypeStruct((NT,) + piece, f32),
        in_specs=[anywhere] * 2 + [vmem] * 4 + [smem] * 3,
        out_specs=vmem,
        scratch_shapes=[
            pltpu.VMEM((R, NG, C, 2) + piece, bf16),
            pltpu.VMEM(field, bf16),
            pltpu.VMEM(field, bf16),
            pltpu.VMEM(field, bf16),
            pltpu.VMEM((n, n, w), f32),
            pltpu.VMEM((w * ld, w), f32),
            pltpu.VMEM((w * ld, w), f32),
            pltpu.VMEM((R, NG, C, 2) + piece, bf16),
            pltpu.VMEM((R, C, NG) + piece, bf16),
            pltpu.VMEM((R, C, NG) + piece, bf16),
            pltpu.VMEM((R, C, NG) + piece, bf16),
            pltpu.VMEM((R, NG) + piece, bf16),
            pltpu.VMEM((NT,) + piece, bf16),
            dma, dma((NT,)), dma((R, NG)), dma((R, C)), dma((R, C)), dma((R, C)), dma((R, C)),
            dma((R, C)), dma((R, C)), dma((R, C)), dma((R, C)), dma((R, NG)), dma((NT,)),
        ],
        compiler_params=pltpu.CompilerParams(
            collective_id=0, has_side_effects=True, vmem_limit_bytes=52 << 20),
    )(targets.reshape((NT,) + piece), partners.reshape(field), *mats, occupations, slot_partner, screening)
    return out.reshape(targets.shape)


def solution(mesh):
    in_specs = (P("tgt", "grp", None, None), P("tgt", None, None, None), P(), P(), P())
    out_specs = P("tgt", "grp", None, None)
    return jax.shard_map(body, mesh=mesh, in_specs=in_specs, out_specs=out_specs, check_vma=False)
```

```python
import functools
import math

import jax
import jax.numpy as jnp
import numpy as np
from jax import lax
from jax.experimental import pallas as pl
from jax.experimental.pallas import tpu as pltpu
from jax.sharding import PartitionSpec as P

coulomb_scale = 0.1
MESH = pl.DeviceIdType.MESH


def tables(points):
    indices = np.arange(points)
    angles = (indices[:, None] * indices[None, :] % points) * (2.0 * math.pi / points)
    norm = 1.0 / math.sqrt(points)
    bf16 = lambda a: a.astype(np.float32).astype(jnp.bfloat16).astype(np.float32)
    return bf16(np.cos(angles) * norm), bf16(np.sin(angles) * norm)


def matrices(points):
    c, s = tables(points)
    n = points
    fz = np.block([[c, -s], [s, c]])
    fz = np.concatenate([fz, fz[:, n:], -fz[:, :n]], axis=1)
    fy = np.block([[c, s], [-s, c]])
    iy = np.block([[c, -s], [s, c]])
    iz = np.block([[c, s], [-s, c]])
    iz = np.concatenate([iz, iz[:, n:], iz[:, :n]], axis=1)
    return [m.astype(jnp.bfloat16) for m in (fz, fy, iy, iz)]


def exchange_kernel(NT, NG, src, part_hbm, fz_ref, fy_ref, iy_ref, iz_ref, occ_ref, slot_ref, scr_ref, out,
                    gat, partner, q1_ref, q2_ref, kern_ref, s1, s2, part, sib, acc, inbox, fin, final,
                    load_sem, p1_send, p1_recv, p2_send, p2_recv, b_send, b_recv,
                    s_send, s_recv, r_send, r_recv, f_send, f_recv):
    f32, bf16 = jnp.float32, jnp.bfloat16
    R, C = NT // NG, NT // 2
    n = kern_ref.shape[0]
    w = 2 * n
    P2 = 2 * src.shape[1]
    k = P2 // n
    ld = s1.shape[0] // w
    t, g = lax.axis_index("tgt"), lax.axis_index("grp")
    c, p = t // 2, t % 2
    own_set = t // R
    sibling = c * 2 + 1 - p
    inside = own_set == g

    load = pltpu.make_async_copy(part_hbm, partner, load_sem)
    load.start()

    barrier = pltpu.get_barrier_semaphore()

    def greet(*device):
        pl.semaphore_signal(barrier, inc=1, device_id=device, device_id_type=MESH)

    for r in range(R):
        for h in range(NG):
            here = (t == g * R + r) & (g == h)
            pl.when(jnp.logical_not(here))(lambda: greet(g * R + r, h))

    @pl.when(inside)
    def _():
        pl.semaphore_wait(barrier, NT - 1)

    @pl.when(jnp.logical_not(inside))
    def _():
        pl.semaphore_wait(barrier, NT)

    def remote(a, b, send, recv, *device):
        return pltpu.make_async_remote_copy(
            src_ref=a, dst_ref=b, send_sem=send, recv_sem=recv, device_id=device, device_id_type=MESH)

    def spread(j):
        return remote(src.at[j], gat.at[t % R, g, j // 2, j % 2], p1_send.at[j], p1_recv.at[t % R, g], j, own_set)

    own_piece = pltpu.make_async_copy(src.at[t], gat.at[t % R, g, c, p], p1_recv.at[t % R, g])
    for m in range(1, NT):
        spread((t + m) % NT).start()
    pl.when(inside)(own_piece.start)
    pl.when(jnp.logical_not(inside))(lambda: spread(t).start())

    def peer(r, m, h):
        ref = gat.at[r, h, c, p]
        return remote(ref, ref, p2_send.at[r, m, h], p2_recv.at[r, m, h], (c + m) % C * 2 + p, g)

    def forward(r, m):
        ref = gat.at[r, :, (c + C - m) % C, p]
        return remote(ref, ref, b_send.at[r, m], b_recv.at[r, m], sibling, g)

    def spread_in_plane(r):
        for d in (0, 1, NG - 1, *range(2, NG - 1)):
            h = (g + d) % NG
            piece = gat.at[r, h, c, p]
            pltpu.make_async_copy(piece, piece, p1_recv.at[r, h]).wait()

            @pl.loop(1, C)
            def _(m):
                peer(r, m, h).start()

        forward(r, 0).start()

    unit = 2.0 * math.pi / n
    kappa = scr_ref[0] * unit
    weight = -occ_ref[slot_ref[t]]
    signed = lambda i: jnp.where(i < n // 2, i, i - n).astype(f32) * unit
    lane = lax.broadcasted_iota(jnp.int32, (n, w), 1)
    gx = signed(lax.broadcasted_iota(jnp.int32, (n, w), 0))
    gz = signed(lane % n)
    base = gx * gx + gz * gz + kappa * kappa

    load.wait()
    low = lax.broadcasted_iota(jnp.int32, (P2, w), 1) < n

    @pl.loop(0, C)
    def _(cc):
        for h in range(NG):
            q = partner[h, cc].astype(f32)
            turned = pltpu.roll(q, n, 1)
            q1_ref[h, cc] = jnp.where(low, q, turned).astype(bf16)
            q2_ref[h, cc] = jnp.where(low, -turned, q).astype(bf16)

    def dot(a, b):
        return jnp.dot(a, b, preferred_element_type=f32)

    def both(ref, h, cc):
        return jnp.concatenate([ref[h, cc], ref[h + 1, cc]], axis=0).astype(f32)

    def stage_one(r, cc):
        @pl.loop(0, NG // 2)
        def _(hh):
            h = hh * 2
            v = jnp.concatenate([gat[r, h, cc].reshape(P2, w), gat[r, h + 1, cc].reshape(P2, w)], axis=0).astype(f32)
            density = (both(q1_ref, h, cc) * v - both(q2_ref, h, cc) * pltpu.roll(v, n, 1)).astype(bf16)
            f = dot(density, fz_ref[...]).astype(bf16)
            for a in range(0, 2 * k, 2):
                stack = [
                    jnp.concatenate([f[b * n:(b + 1) * n, :w], f[b * n:(b + 1) * n, w:]], axis=0)
                    for b in (a, a + 1)
                ]
                o = dot(fy_ref[...], jnp.concatenate(stack, axis=1))
                for b in range(2):
                    x = ((h + (a + b) // k) * C + cc) * k + (a + b) % k
                    s1[pl.ds(x, w, stride=ld), :] = o[:, b * w:(b + 1) * w]

    def rows_of(s, i):
        top = s[pl.ds(pl.multiple_of(i * ld, 8), n), :]
        bottom = s[pl.ds(pl.multiple_of((i + n) * ld, 8), n), :]
        return jnp.concatenate([top, bottom], axis=0).astype(bf16)

    def stage_two():
        G = 8

        @pl.loop(0, n // G)
        def _(i):
            for a in range(0, G, 2):
                ky = i * G + a
                spectrum = dot(fy_ref[...], jnp.concatenate([rows_of(s1, ky), rows_of(s1, ky + 1)], axis=1))
                half = jnp.concatenate([kern_ref[ky], kern_ref[ky + 1]], axis=1)
                scaled = (spectrum * jnp.concatenate([half, half], axis=0)).astype(bf16)
                o = dot(iy_ref[...], scaled)
                for b in range(2):
                    s2[pl.ds(ky + b, w, stride=ld), :] = o[:, b * w:(b + 1) * w]

    def stage_three(r, cc):
        @pl.loop(0, NG // 2)
        def _(hh):
            h = hh * 2
            parts = []
            for a in range(0, 2 * k, 2):
                stack = [
                    rows_of(s2, ((h + e // k) * C + cc) * k + e % k) for e in (a, a + 1)
                ]
                o = dot(iy_ref[:n, :], jnp.concatenate(stack, axis=1)).astype(bf16)
                parts += [o[:, :w], o[:, w:]]
            potential = dot(jnp.concatenate(parts, axis=0), iz_ref[...])
            result = weight * (potential[:, :w] * both(q1_ref, h, cc) + potential[:, w:] * both(q2_ref, h, cc))
            result = result.astype(bf16)
            part[r, h, cc] = result[:P2].reshape(2, P2 // 2, w)
            part[r, h + 1, cc] = result[P2:].reshape(2, P2 // 2, w)

    def out_sibling(r, m):
        return remote(part.at[r, :, (c + m) % C, 1 - p], sib.at[r, m], s_send.at[r, m], s_recv.at[r, m], sibling, g)

    def out_peer(r, m, h):
        return remote(acc.at[r, m, h], inbox.at[r, m, h], r_send.at[r, m, h], r_recv.at[r, m, h],
                      (c + m) % C * 2 + p, g)

    def send_peer(r, m):
        for d in range(1, NG + 1):
            out_peer(r, m, (g + d) % NG).start()

    def to_owner(r, h):
        return remote(fin.at[r, h], final.at[t], f_send.at[r, h], f_recv.at[t], g * R + r, h)

    def add_sibling(r, m):
        out_sibling(r, m).wait_recv()
        mine = part[r, :, (c + m) % C, p]
        acc[r, m] = (mine.astype(f32) + sib[r, m].astype(f32)).astype(bf16)

    own_sum = pltpu.make_async_copy(fin.at[t % R, g], final.at[t], f_recv.at[t])

    def finish(r):
        for d in range(1, NG + 1):
            h = (g + d) % NG
            total = acc[r, 0, h].astype(f32)
            for m in range(1, C):
                out_peer(r, m, h).wait_recv()
                total = total + inbox[r, m, h].astype(f32)
            fin[r, h] = total.astype(bf16)
            here = (t == g * R + r) & (g == h)
            pl.when(here)(own_sum.start)
            pl.when(jnp.logical_not(here))(lambda: to_owner(r, h).start())

    for r in range(R):
        spread_in_plane(r)

    @pl.loop(0, n)
    def _(ky):
        gy = signed(ky)
        kern_ref[ky] = coulomb_scale / (base + gy * gy)

    for r in range(R):

        @pl.loop(1, C)
        def _(m):
            for h in range(NG):
                peer(r, m, h).wait_recv()
            forward(r, m).start()
            forward(r, m - 1).wait_recv()
            stage_one(r, (c + C - (m - 1)) % C)

        forward(r, C - 1).wait_recv()
        stage_one(r, (c + 1) % C)
        if r:
            finish(r - 1)
        stage_two()

        stage_three(r, (c + 1) % C)
        out_sibling(r, 1).start()

        @pl.loop(2, C)
        def _(m):
            stage_three(r, (c + m) % C)
            out_sibling(r, m).start()
            add_sibling(r, m - 1)
            send_peer(r, m - 1)

        stage_three(r, c)
        out_sibling(r, 0).start()
        add_sibling(r, C - 1)
        send_peer(r, C - 1)
        add_sibling(r, 0)
    finish(R - 1)

    for m in range(NT):
        j = (t + m) % NT
        piece = final.at[j]
        pltpu.make_async_copy(piece, piece, f_recv.at[j]).wait()
        out[j] = final[j].astype(f32)
    for m in range(1, NT):
        spread((t + m) % NT).wait_send()
    pl.when(jnp.logical_not(inside))(lambda: spread(t).wait_send())
    for r in range(R):
        for m in range(C):
            forward(r, m).wait_send()
            out_sibling(r, m).wait_send()
            for h in range(NG if m else 0):
                peer(r, m, h).wait_send()
                out_peer(r, m, h).wait_send()
        for h in range(NG):
            here = (t == g * R + r) & (g == h)
            pl.when(jnp.logical_not(here))(lambda: to_owner(r, h).wait_send())


def body(targets, partners, occupations, slot_partner, screening):
    NT, NG = lax.axis_size("tgt"), lax.axis_size("grp")
    R, C = NT // NG, NT // 2
    _, planes, n, w = targets.shape
    rows = planes * n // NT
    piece = (rows, w)
    anywhere = pl.BlockSpec(memory_space=pl.ANY)
    vmem = pl.BlockSpec(memory_space=pltpu.VMEM)
    smem = pl.BlockSpec(memory_space=pltpu.SMEM)
    dma = pltpu.SemaphoreType.DMA
    bf16, f32 = jnp.bfloat16, jnp.float32
    mats = [jnp.asarray(m) for m in matrices(n)]
    ld = n + 8
    field = (NG, C, 2 * rows, w)
    out = pl.pallas_call(
        functools.partial(exchange_kernel, NT, NG),
        out_shape=jax.ShapeDtypeStruct((NT,) + piece, f32),
        in_specs=[anywhere] * 2 + [vmem] * 4 + [smem] * 3,
        out_specs=vmem,
        scratch_shapes=[
            pltpu.VMEM((R, NG, C, 2) + piece, bf16),
            pltpu.VMEM(field, bf16),
            pltpu.VMEM(field, bf16),
            pltpu.VMEM(field, bf16),
            pltpu.VMEM((n, n, w), f32),
            pltpu.VMEM((w * ld, w), f32),
            pltpu.VMEM((w * ld, w), f32),
            pltpu.VMEM((R, NG, C, 2) + piece, bf16),
            pltpu.VMEM((R, C, NG) + piece, bf16),
            pltpu.VMEM((R, C, NG) + piece, bf16),
            pltpu.VMEM((R, C, NG) + piece, bf16),
            pltpu.VMEM((R, NG) + piece, bf16),
            pltpu.VMEM((NT,) + piece, bf16),
            dma, dma((NT,)), dma((R, NG)), dma((R, C, NG)), dma((R, C, NG)), dma((R, C)), dma((R, C)),
            dma((R, C)), dma((R, C)), dma((R, C, NG)), dma((R, C, NG)), dma((R, NG)), dma((NT,)),
        ],
        compiler_params=pltpu.CompilerParams(
            collective_id=0, has_side_effects=True, vmem_limit_bytes=52 << 20),
    )(targets.reshape((NT,) + piece), partners.reshape(field), *mats, occupations, slot_partner, screening)
    return out.reshape(targets.shape)


def solution(mesh):
    in_specs = (P("tgt", "grp", None, None), P("tgt", None, None, None), P(), P(), P())
    out_specs = P("tgt", "grp", None, None)
    return jax.shard_map(body, mesh=mesh, in_specs=in_specs, out_specs=out_specs, check_vma=False)
```

```python
import functools
import math

import jax
import jax.numpy as jnp
import numpy as np
from jax import lax
from jax.experimental import pallas as pl
from jax.experimental.pallas import tpu as pltpu
from jax.sharding import PartitionSpec as P

coulomb_scale = 0.1
MESH = pl.DeviceIdType.MESH


def tables(points):
    indices = np.arange(points)
    angles = (indices[:, None] * indices[None, :] % points) * (2.0 * math.pi / points)
    norm = 1.0 / math.sqrt(points)
    bf16 = lambda a: a.astype(np.float32).astype(jnp.bfloat16).astype(np.float32)
    return bf16(np.cos(angles) * norm), bf16(np.sin(angles) * norm)


def matrices(points):
    c, s = tables(points)
    n = points
    fz = np.block([[c, -s], [s, c]])
    fz = np.concatenate([fz, fz[:, n:], -fz[:, :n]], axis=1)
    fy = np.block([[c, s], [-s, c]])
    iy = np.block([[c, -s], [s, c]])
    iz = np.block([[c, s], [-s, c]])
    iz = np.concatenate([iz, iz[:, n:], iz[:, :n]], axis=1)
    return [m.astype(jnp.bfloat16) for m in (fz, fy, iy, iz)]


def exchange_kernel(NT, NG, src, part_hbm, fz_ref, fy_ref, iy_ref, iz_ref, occ_ref, slot_ref, scr_ref, out,
                    mid, gat, partner, q1_ref, q2_ref, kern_ref, s1, s2, part, sib, acc, inbox, fin, final,
                    load_sem, p0_send, p0_recv, p1_send, p1_recv, p2_send, p2_recv, b_send, b_recv,
                    s_send, s_recv, r_send, r_recv, f_send, f_recv):
    f32, bf16 = jnp.float32, jnp.bfloat16
    R, C = NT // NG, NT // 2
    n = kern_ref.shape[0]
    w = 2 * n
    P2 = 2 * src.shape[1]
    k = P2 // n
    ld = s1.shape[0] // w
    t, g = lax.axis_index("tgt"), lax.axis_index("grp")
    c, p = t // 2, t % 2
    sibling = c * 2 + 1 - p

    load = pltpu.make_async_copy(part_hbm, partner, load_sem)
    load.start()

    barrier = pltpu.get_barrier_semaphore()

    def greet(*device):
        pl.semaphore_signal(barrier, inc=1, device_id=device, device_id_type=MESH)

    for m in range(1, NT):
        greet((t + m) % NT, g)
    for d in range(1, NG):
        greet(t, (g + d) % NG)
    pl.semaphore_wait(barrier, NT + NG - 2)

    def remote(a, b, send, recv, *device):
        return pltpu.make_async_remote_copy(
            src_ref=a, dst_ref=b, send_sem=send, recv_sem=recv, device_id=device, device_id_type=MESH)

    def spread(j):
        return remote(src.at[j], mid.at[t], p0_send.at[j], p0_recv.at[t], j, g)

    def along(h, r):
        return remote(mid.at[h * R + r], gat.at[r, g, c, p], p1_send.at[h, r], p1_recv.at[r, g], t, h)

    own_piece = pltpu.make_async_copy(src.at[t], mid.at[t], p0_recv.at[t])
    for m in range(1, NT):
        spread((t + m) % NT).start()
    own_piece.start()
    for d in (*range(1, NG), 0):
        h = (g + d) % NG
        for r in range(R):
            pltpu.make_async_copy(mid.at[h * R + r], mid.at[h * R + r], p0_recv.at[h * R + r]).wait()
            if d:
                along(h, r).start()
            else:
                pltpu.make_async_copy(mid.at[g * R + r], gat.at[r, g, c, p], p1_recv.at[r, g]).start()

    def peer(r, m, h):
        ref = gat.at[r, h, c, p]
        return remote(ref, ref, p2_send.at[r, m, h], p2_recv.at[r, m, h], (c + m) % C * 2 + p, g)

    def forward(r, m):
        ref = gat.at[r, :, (c + C - m) % C, p]
        return remote(ref, ref, b_send.at[r, m], b_recv.at[r, m], sibling, g)

    def spread_in_plane(r):
        for d in (0, 1, NG - 1, *range(2, NG - 1)):
            h = (g + d) % NG
            piece = gat.at[r, h, c, p]
            pltpu.make_async_copy(piece, piece, p1_recv.at[r, h]).wait()

            @pl.loop(1, C)
            def _(m):
                peer(r, m, h).start()

        forward(r, 0).start()

    unit = 2.0 * math.pi / n
    kappa = scr_ref[0] * unit
    weight = -occ_ref[slot_ref[t]]
    signed = lambda i: jnp.where(i < n // 2, i, i - n).astype(f32) * unit
    lane = lax.broadcasted_iota(jnp.int32, (n, w), 1)
    gx = signed(lax.broadcasted_iota(jnp.int32, (n, w), 0))
    gz = signed(lane % n)
    base = gx * gx + gz * gz + kappa * kappa

    load.wait()
    low = lax.broadcasted_iota(jnp.int32, (P2, w), 1) < n

    @pl.loop(0, C)
    def _(cc):
        for h in range(NG):
            q = partner[h, cc].astype(f32)
            turned = pltpu.roll(q, n, 1)
            q1_ref[h, cc] = jnp.where(low, q, turned).astype(bf16)
            q2_ref[h, cc] = jnp.where(low, -turned, q).astype(bf16)

    def dot(a, b):
        return jnp.dot(a, b, preferred_element_type=f32)

    def both(ref, h, cc):
        return jnp.concatenate([ref[h, cc], ref[h + 1, cc]], axis=0).astype(f32)

    def stage_one(r, cc):
        @pl.loop(0, NG // 2)
        def _(hh):
            h = hh * 2
            v = jnp.concatenate([gat[r, h, cc].reshape(P2, w), gat[r, h + 1, cc].reshape(P2, w)], axis=0).astype(f32)
            density = (both(q1_ref, h, cc) * v - both(q2_ref, h, cc) * pltpu.roll(v, n, 1)).astype(bf16)
            f = dot(density, fz_ref[...]).astype(bf16)
            for a in range(0, 2 * k, 2):
                stack = [
                    jnp.concatenate([f[b * n:(b + 1) * n, :w], f[b * n:(b + 1) * n, w:]], axis=0)
                    for b in (a, a + 1)
                ]
                o = dot(fy_ref[...], jnp.concatenate(stack, axis=1))
                for b in range(2):
                    x = ((h + (a + b) // k) * C + cc) * k + (a + b) % k
                    s1[pl.ds(x, w, stride=ld), :] = o[:, b * w:(b + 1) * w]

    def rows_of(s, i):
        top = s[pl.ds(pl.multiple_of(i * ld, 8), n), :]
        bottom = s[pl.ds(pl.multiple_of((i + n) * ld, 8), n), :]
        return jnp.concatenate([top, bottom], axis=0).astype(bf16)

    def stage_two():
        G = 8

        @pl.loop(0, n // G)
        def _(i):
            for a in range(0, G, 2):
                ky = i * G + a
                spectrum = dot(fy_ref[...], jnp.concatenate([rows_of(s1, ky), rows_of(s1, ky + 1)], axis=1))
                half = jnp.concatenate([kern_ref[ky], kern_ref[ky + 1]], axis=1)
                scaled = (spectrum * jnp.concatenate([half, half], axis=0)).astype(bf16)
                o = dot(iy_ref[...], scaled)
                for b in range(2):
                    s2[pl.ds(ky + b, w, stride=ld), :] = o[:, b * w:(b + 1) * w]

    def stage_three(r, cc):
        @pl.loop(0, NG // 2)
        def _(hh):
            h = hh * 2
            parts = []
            for a in range(0, 2 * k, 2):
                stack = [
                    rows_of(s2, ((h + e // k) * C + cc) * k + e % k) for e in (a, a + 1)
                ]
                o = dot(iy_ref[:n, :], jnp.concatenate(stack, axis=1)).astype(bf16)
                parts += [o[:, :w], o[:, w:]]
            potential = dot(jnp.concatenate(parts, axis=0), iz_ref[...])
            result = weight * (potential[:, :w] * both(q1_ref, h, cc) + potential[:, w:] * both(q2_ref, h, cc))
            result = result.astype(bf16)
            part[r, h, cc] = result[:P2].reshape(2, P2 // 2, w)
            part[r, h + 1, cc] = result[P2:].reshape(2, P2 // 2, w)

    def out_sibling(r, m):
        return remote(part.at[r, :, (c + m) % C, 1 - p], sib.at[r, m], s_send.at[r, m], s_recv.at[r, m], sibling, g)

    def out_peer(r, m, h):
        return remote(acc.at[r, m, h], inbox.at[r, m, h], r_send.at[r, m, h], r_recv.at[r, m, h],
                      (c + m) % C * 2 + p, g)

    def send_peer(r, m):
        for d in range(1, NG + 1):
            out_peer(r, m, (g + d) % NG).start()

    def to_owner(r, h):
        return remote(fin.at[r, h], final.at[t], f_send.at[r, h], f_recv.at[t], g * R + r, h)

    def add_sibling(r, m):
        out_sibling(r, m).wait_recv()
        mine = part[r, :, (c + m) % C, p]
        acc[r, m] = (mine.astype(f32) + sib[r, m].astype(f32)).astype(bf16)

    own_sum = pltpu.make_async_copy(fin.at[t % R, g], final.at[t], f_recv.at[t])

    def finish(r):
        for d in range(1, NG + 1):
            h = (g + d) % NG
            total = acc[r, 0, h].astype(f32)
            for m in range(1, C):
                out_peer(r, m, h).wait_recv()
                total = total + inbox[r, m, h].astype(f32)
            fin[r, h] = total.astype(bf16)
            here = (t == g * R + r) & (g == h)
            pl.when(here)(own_sum.start)
            pl.when(jnp.logical_not(here))(lambda: to_owner(r, h).start())

    for r in range(R):
        spread_in_plane(r)

    @pl.loop(0, n)
    def _(ky):
        gy = signed(ky)
        kern_ref[ky] = coulomb_scale / (base + gy * gy)

    for r in range(R):

        @pl.loop(1, C)
        def _(m):
            for h in range(NG):
                peer(r, m, h).wait_recv()
            forward(r, m).start()
            forward(r, m - 1).wait_recv()
            stage_one(r, (c + C - (m - 1)) % C)

        forward(r, C - 1).wait_recv()
        stage_one(r, (c + 1) % C)
        if r:
            finish(r - 1)
        stage_two()

        stage_three(r, (c + 1) % C)
        out_sibling(r, 1).start()

        @pl.loop(2, C)
        def _(m):
            stage_three(r, (c + m) % C)
            out_sibling(r, m).start()
            add_sibling(r, m - 1)
            send_peer(r, m - 1)

        stage_three(r, c)
        out_sibling(r, 0).start()
        add_sibling(r, C - 1)
        send_peer(r, C - 1)
        add_sibling(r, 0)
    finish(R - 1)

    for m in range(NT):
        j = (t + m) % NT
        piece = final.at[j]
        pltpu.make_async_copy(piece, piece, f_recv.at[j]).wait()
        out[j] = final[j].astype(f32)
    for m in range(1, NT):
        spread((t + m) % NT).wait_send()
    for d in range(1, NG):
        for r in range(R):
            along((g + d) % NG, r).wait_send()
    for r in range(R):
        for m in range(C):
            forward(r, m).wait_send()
            out_sibling(r, m).wait_send()
            for h in range(NG if m else 0):
                peer(r, m, h).wait_send()
                out_peer(r, m, h).wait_send()
        for h in range(NG):
            here = (t == g * R + r) & (g == h)
            pl.when(jnp.logical_not(here))(lambda: to_owner(r, h).wait_send())


def body(targets, partners, occupations, slot_partner, screening):
    NT, NG = lax.axis_size("tgt"), lax.axis_size("grp")
    R, C = NT // NG, NT // 2
    _, planes, n, w = targets.shape
    rows = planes * n // NT
    piece = (rows, w)
    anywhere = pl.BlockSpec(memory_space=pl.ANY)
    vmem = pl.BlockSpec(memory_space=pltpu.VMEM)
    smem = pl.BlockSpec(memory_space=pltpu.SMEM)
    dma = pltpu.SemaphoreType.DMA
    bf16, f32 = jnp.bfloat16, jnp.float32
    mats = [jnp.asarray(m) for m in matrices(n)]
    ld = n + 8
    field = (NG, C, 2 * rows, w)
    out = pl.pallas_call(
        functools.partial(exchange_kernel, NT, NG),
        out_shape=jax.ShapeDtypeStruct((NT,) + piece, f32),
        in_specs=[anywhere] * 2 + [vmem] * 4 + [smem] * 3,
        out_specs=vmem,
        scratch_shapes=[
            pltpu.VMEM((NT,) + piece, bf16),
            pltpu.VMEM((R, NG, C, 2) + piece, bf16),
            pltpu.VMEM(field, bf16),
            pltpu.VMEM(field, bf16),
            pltpu.VMEM(field, bf16),
            pltpu.VMEM((n, n, w), f32),
            pltpu.VMEM((w * ld, w), f32),
            pltpu.VMEM((w * ld, w), f32),
            pltpu.VMEM((R, NG, C, 2) + piece, bf16),
            pltpu.VMEM((R, C, NG) + piece, bf16),
            pltpu.VMEM((R, C, NG) + piece, bf16),
            pltpu.VMEM((R, C, NG) + piece, bf16),
            pltpu.VMEM((R, NG) + piece, bf16),
            pltpu.VMEM((NT,) + piece, bf16),
            dma, dma((NT,)), dma((NT,)), dma((NG, R)), dma((R, NG)), dma((R, C, NG)), dma((R, C, NG)), dma((R, C)), dma((R, C)),
            dma((R, C)), dma((R, C)), dma((R, C, NG)), dma((R, C, NG)), dma((R, NG)), dma((NT,)),
        ],
        compiler_params=pltpu.CompilerParams(
            collective_id=0, has_side_effects=True, vmem_limit_bytes=52 << 20),
    )(targets.reshape((NT,) + piece), partners.reshape(field), *mats, occupations, slot_partner, screening)
    return out.reshape(targets.shape)


def solution(mesh):
    in_specs = (P("tgt", "grp", None, None), P("tgt", None, None, None), P(), P(), P())
    out_specs = P("tgt", "grp", None, None)
    return jax.shard_map(body, mesh=mesh, in_specs=in_specs, out_specs=out_specs, check_vma=False)
```
